256 devices in a mesh: row: 8 (over z), col: 8 (over x, core), depth: 4 (over y).
Axes of the slice: x: 4, y: 4, z: 8, core: 2. Of those that a mesh axis runs over, the one named last changes fastest.
Arguments:
- amplitudes: bfloat16 [6400, 7200], P('row', ('col', 'depth')), may hold values from -6 to 6
- integrals: bfloat16 [7200, 16384], P('row', ('col', 'depth')), may hold values from -0.0625 to 0.0625
- cycle_integrals: bfloat16 [512, 512], P('row'), as said below
- occ_irrep: int32 [100], replicated, may hold values from 0 to 7
- vir_irrep: int32 [900], replicated, may hold values from 0 to 7
Outputs:
- ladder: bfloat16 [6400, 16384], P('row', ('col', 'depth'))
- cycle: bfloat16 [512, 57600], P('row', ('col', 'depth'))
The draws below stay inside these ranges and needn't reach their ends.
Inputs may be any that keep to these rules, and one draw needn't show every extreme that they name: cycle_integrals equals its transpose.
All inputs are finite; a program needn't handle non-finite values.
Results may differ from the reference program's by a relative error of at most 0.001.
Values may be sent and summed in bfloat16 or wider, within the bound.
No kernel may reach another device: no remote copies, remote signals or barrier semaphores. Data moves between devices by JAX's collectives and lax.ppermute only.
A program may use at most 128 MiB of HBM per device.

```python
import math
import jax
import jax.numpy as jnp

NO = 100
NV = 900
BW = 512
JW = 64
CW = 8
IW = 64
AW = 32
K = 7200


def draw_cycle_integrals(key, part):
    entries = IW * CW
    sample = jax.random.normal(key, (entries, entries), jnp.float32)
    return ((sample + sample.T) * (0.70710678 / math.sqrt(entries))).astype(jnp.bfloat16)


def set_ends(values, own_key, smallest, top_value):
    place = [jax.random.randint(jax.random.fold_in(own_key, axis), (), 0, length) for axis, length in enumerate(values.shape)]
    longest = values.shape.index(max(values.shape))
    beside = place[:longest] + [(place[longest] + 1) % values.shape[longest]] + place[longest + 1:]
    return values.at[tuple(place)].set(smallest).at[tuple(beside)].set(top_value)


def block_levels(stream_key, shape, cuts, least, top_value):
    gain, own = 1.0, jax.random.fold_in(stream_key, 6)
    for axis_at, shards_of in cuts:
        steps = jnp.exp(jax.random.uniform(jax.random.fold_in(own, axis_at), (shards_of,), jnp.float32, least / len(cuts), top_value / len(cuts)))
        gain = gain * jnp.repeat(steps, shape[axis_at] // shards_of).reshape([-1 if axis == axis_at else 1 for axis in range(len(shape))])
    return gain


def normal_values(rng, dims, scale, most, split=(), dtype=jnp.bfloat16):
    factor_of = block_levels(rng, dims, split, -0.22, 0.18) if split else 1.0
    result = jax.random.normal(rng, dims, jnp.float32) * scale * factor_of
    return jnp.minimum(jnp.maximum(result, -most), most).astype(dtype)


def setup_inputs(seed: int = 0) -> dict:
    keys = jax.random.split(jax.random.key(seed), 6)
    return {
        "amplitudes": normal_values(keys[0], (IW * NO, K), 1.0, 6.0, ((0, 8), (1, 32))),
        "integrals": normal_values(keys[1], (K, AW * BW), K ** -0.5, 0.0625, ((0, 8), (1, 32))),
        "cycle_integrals": draw_cycle_integrals(jax.random.fold_in(keys[5], 71), 0),
        "occ_irrep": set_ends(jax.random.randint(keys[3], (NO,), 0, 8), jax.random.fold_in(keys[3], 1), 0, 7).astype(jnp.int32),
        "vir_irrep": set_ends(jax.random.randint(keys[4], (NV,), 0, 8), jax.random.fold_in(keys[4], 1), 0, 7).astype(jnp.int32),
    }


def label_bits(labels):
    return jnp.stack([labels % 2, (labels // 2) % 2, (labels // 4) % 2])


def reference(amplitudes, integrals, cycle_integrals, occ_irrep, vir_irrep):
    ladder = jnp.dot(amplitudes, integrals, preferred_element_type=jnp.float32).astype(jnp.bfloat16)
    regrouped = amplitudes.reshape(IW, NO, CW, NV)[:, :JW].transpose(0, 2, 1, 3).reshape(IW * CW, JW * NV)
    cycle_sum = jnp.dot(cycle_integrals, regrouped, preferred_element_type=jnp.float32)
    occ_bits = label_bits(occ_irrep)
    vir_bits = label_bits(vir_irrep)
    odd_count = jnp.zeros((IW * CW, JW * NV), jnp.int32)
    for digit in range(3):
        row_bits = (occ_bits[digit, :IW, None] + vir_bits[digit, None, :CW]).reshape(IW * CW)
        column_bits = (occ_bits[digit, :JW, None] + vir_bits[digit, None, :]).reshape(JW * NV)
        odd_count = odd_count + (row_bits[:, None] + column_bits[None, :]) % 2
    cycle = jnp.where(odd_count == 0, cycle_sum, jnp.float32(0.0)).astype(jnp.bfloat16)
    return ladder, cycle
```

```python
import functools

import jax
import jax.numpy as jnp
from jax import lax
from jax.experimental import pallas as pl
from jax.experimental.pallas import tpu as pltpu
from jax.sharding import PartitionSpec as P

NO = 100
NV = 900
JW = 64
CW = 8
RING = 8
QUARTERS = 4
UP = [(i, (i + 1) % RING) for i in range(RING)]
DOWN = [(i, (i - 1) % RING) for i in range(RING)]


def shift(value, step):
    return lax.ppermute(value, "row", UP if step > 0 else DOWN)


def ladder_kernel(n, first, last, owner_ref, amps_ref, *refs):
    blocks = refs[: 2 * n]
    refs = refs[2 * n :]
    before_ref = None
    if not first:
        before_ref, refs = refs[0], refs[1:]
    out_ref, held, sems = refs[0], refs[1], refs[2]
    total = refs[3] if last and n > 1 else out_ref

    def fetch(k):
        start = pl.multiple_of(owner_ref[k] * QUARTERS, QUARTERS)
        return pltpu.make_async_copy(
            amps_ref.at[pl.ds(start, QUARTERS)], held.at[k % 2], sems.at[k % 2]
        )

    fetch(0).start()
    for k in range(n):
        fetch(k).wait()
        if k + 1 < n:
            fetch(k + 1).start()

        def tile(m, _, k=k):
            rows = pl.ds(pl.multiple_of(m * 400, 400), 400)
            value = None
            for q in range(QUARTERS):
                term = jnp.dot(
                    held[k % 2, q, rows, :],
                    blocks[2 * k + q // 2][q % 2],
                    preferred_element_type=jnp.float32,
                )
                value = term if value is None else value + term
            if k > 0:
                value = value + total[rows, :]
            elif before_ref is not None:
                value = value + before_ref[rows, :]
            if last and k == n - 1:
                out_ref[rows, :] = value.astype(out_ref.dtype)
            else:
                total[rows, :] = value
            return 0

        lax.fori_loop(0, 2, tile, 0)


def ladder_part(owners, amps, blocks, before, last):
    n = len(blocks) // 2
    rows, columns = amps.shape[1], blocks[0].shape[2]
    first = before is None
    scratch = [
        pltpu.VMEM((2, QUARTERS) + amps.shape[1:], jnp.bfloat16),
        pltpu.SemaphoreType.DMA((2,)),
    ]
    if last and n > 1:
        scratch.append(pltpu.VMEM((rows, columns), jnp.float32))
    whole = pl.BlockSpec(memory_space=pltpu.VMEM)
    return pl.pallas_call(
        functools.partial(ladder_kernel, n, first, last),
        out_shape=jax.ShapeDtypeStruct((rows, columns), jnp.bfloat16 if last else jnp.float32),
        in_specs=[pl.BlockSpec(memory_space=pltpu.SMEM), pl.BlockSpec(memory_space=pl.ANY)]
        + [whole] * (2 * n + (0 if first else 1)),
        out_specs=whole,
        scratch_shapes=scratch,
        compiler_params=pltpu.CompilerParams(vmem_limit_bytes=40 << 20),
        cost_estimate=pl.CostEstimate(
            flops=2 * rows * NV * columns * n,
            bytes_accessed=2 * n * NV * (rows + columns),
            transcendentals=0,
        ),
    )(owners, amps, *blocks, *([] if first else [before]))


def shards(amplitudes, integrals, cycle_integrals, occ_irrep, vir_irrep):
    rows_here, local_cols = amplitudes.shape
    occ_block = rows_here // NO
    z = lax.axis_index("row")
    p = lax.axis_index(("col", "depth"))

    gathered = lax.all_gather(amplitudes, ("col", "depth"), axis=0, tiled=True)
    gathered = gathered.reshape(RING * QUARTERS, rows_here, local_cols)

    half = NV // 2
    top = integrals[:half].reshape(2, half // 2, -1)
    bot = integrals[half:].reshape(2, half // 2, -1)

    regroup_in = amplitudes.reshape(occ_block, NO, local_cols)[:, :JW, :]
    spread = lax.all_to_all(regroup_in, ("col", "depth"), split_axis=1, concat_axis=2, tiled=True)
    occ_here = spread.shape[1]
    columns = occ_here * NV
    ordered = (
        spread.reshape(occ_block, occ_here, CW, NV)
        .transpose(0, 2, 1, 3)
        .reshape(occ_block * CW, columns)
    )

    tops, bots, regrouped = {0: top}, {0: bot}, {0: ordered}
    for s in range(1, 5):
        tops[-s] = shift(tops[1 - s], 1)
        bots[s] = shift(bots[s - 1], -1)
        if s < 4:
            bots[-s] = shift(bots[1 - s], 1)
            tops[s] = shift(tops[s - 1], -1)
            regrouped[-s] = shift(regrouped[1 - s], 1)
            regrouped[s] = shift(regrouped[s - 1], -1)
    tops[4] = tops.pop(-4)
    width = ordered.shape[0] // 2
    regrouped[4] = jnp.concatenate(
        [shift(regrouped[-3][:width], 1), shift(regrouped[3][width:], -1)], axis=0
    )

    def blocks(offsets):
        return [b for d in offsets for b in (tops[d], bots[d])]

    def owners(offsets):
        return jnp.stack([(z + d) % RING for d in offsets]).astype(jnp.int32)

    early, late = [0, -1, 1, -2, 2, -3, 3], [4]
    total = ladder_part(owners(early), gathered, blocks(early), None, False)
    ladder = ladder_part(owners(late), gathered, blocks(late), total, True)

    rel = list(range(RING))
    stacked = jnp.concatenate([regrouped[d if d <= 4 else d - RING] for d in rel], axis=0)
    per_row = cycle_integrals.shape[1] // RING
    twice = jnp.concatenate([cycle_integrals, cycle_integrals], axis=1)
    rolled = lax.dynamic_slice_in_dim(twice, z * per_row, RING * per_row, axis=1)
    cycle_sum = jnp.dot(rolled, stacked, preferred_element_type=jnp.float32)

    rows_cycle = cycle_integrals.shape[0]
    occ_rows = lax.dynamic_slice_in_dim(occ_irrep, z * (rows_cycle // CW), rows_cycle // CW)
    row_label = ((occ_rows[:, None] ^ vir_irrep[None, :CW]) & 7).reshape(rows_cycle)
    occ_cols = lax.dynamic_slice_in_dim(occ_irrep, p * occ_here, occ_here)
    col_label = ((occ_cols[:, None] ^ vir_irrep[None, :]) & 7).reshape(columns)
    allowed = row_label[:, None] == col_label[None, :]
    cycle = jnp.where(allowed, cycle_sum, jnp.float32(0.0)).astype(jnp.bfloat16)
    return ladder, cycle


def solution(mesh):
    in_specs = (P("row", ("col", "depth")), P("row", ("col", "depth")), P("row", None), P(), P())
    out_specs = (P("row", ("col", "depth")), P("row", ("col", "depth")))
    return jax.shard_map(shards, mesh=mesh, in_specs=in_specs, out_specs=out_specs, check_vma=False)
```

```python
import functools

import jax
import jax.numpy as jnp
from jax import lax
from jax.experimental import pallas as pl
from jax.experimental.pallas import tpu as pltpu
from jax.sharding import PartitionSpec as P

NO = 100
NV = 900
JW = 64
CW = 8
RING = 8
QUARTERS = 4
LANES = 256
OFFSETS = (0, -1, 1, -2, 2, -3, 3, 4, 4)
UP = [(i, (i + 1) % RING) for i in range(RING)]
DOWN = [(i, (i - 1) % RING) for i in range(RING)]
WHOLE = pl.BlockSpec(memory_space=pltpu.VMEM)


def shift(value, step):
    return lax.ppermute(value, "row", UP if step > 0 else DOWN)


def tie(value, done):
    at = (0,) * value.ndim
    size = (1,) * (value.ndim - 2) + (8, 128)
    corner = lax.slice(value, at, size)
    for other in done:
        first = lax.slice(other, (0,) * other.ndim, (1,) * (other.ndim - 2) + (8, 128))
        corner = corner + first.reshape(size) * jnp.zeros((), value.dtype)
    return lax.dynamic_update_slice(value, corner, at)


def ladder_kernel(n, first, last, owner_ref, amps_ref, *refs):
    blocks, refs = refs[: 2 * n], refs[2 * n :]
    before_ref = None
    if not first:
        before_ref, refs = refs[0], refs[1:]
    out_ref, held, halves, right, sems = refs[:5]
    total = refs[5] if last and n > 1 else out_ref

    def fetch(k):
        start = pl.multiple_of(owner_ref[k] * QUARTERS, QUARTERS)
        copies = [
            pltpu.make_async_copy(
                amps_ref.at[start + q],
                held.at[k % 2, :, pl.ds(LANES * q, LANES)],
                sems.at[k % 2, q],
            )
            for q in range(QUARTERS)
        ]
        copies += [
            pltpu.make_async_copy(blocks[2 * k + h], halves.at[k % 2, h], sems.at[k % 2, QUARTERS + h])
            for h in range(2)
        ]
        return copies

    for c in fetch(0):
        c.start()
    for k in range(n):
        if k + 1 < n:
            for c in fetch(k + 1):
                c.start()
        for c in fetch(k):
            c.wait()
        for q in range(QUARTERS):
            block = halves[k % 2, q // 2, q % 2]
            rest = jnp.zeros((LANES - block.shape[0], block.shape[1]), block.dtype)
            right[LANES * q : LANES * (q + 1), :] = jnp.concatenate([block, rest], axis=0)
        value = jnp.dot(held[k % 2], right[...], preferred_element_type=jnp.float32)
        if k > 0:
            value = value + total[...]
        elif before_ref is not None:
            value = value + before_ref[...]
        if last and k == n - 1:
            out_ref[...] = value.astype(out_ref.dtype)
        else:
            total[...] = value


def ladder_part(owners, amps, blocks, before, last):
    n = len(blocks) // 2
    rows, columns = amps.shape[1], blocks[0].shape[2]
    first = before is None
    depth = QUARTERS * LANES
    scratch = [
        pltpu.VMEM((2, rows, depth), jnp.bfloat16),
        pltpu.VMEM((2, 2) + blocks[0].shape, jnp.bfloat16),
        pltpu.VMEM((depth, columns), jnp.bfloat16),
        pltpu.SemaphoreType.DMA((2, QUARTERS + 2)),
    ]
    if last and n > 1:
        scratch.append(pltpu.VMEM((rows, columns), jnp.float32))
    return pl.pallas_call(
        functools.partial(ladder_kernel, n, first, last),
        out_shape=jax.ShapeDtypeStruct((rows, columns), jnp.bfloat16 if last else jnp.float32),
        in_specs=[pl.BlockSpec(memory_space=pltpu.SMEM), pl.BlockSpec(memory_space=pl.ANY)]
        + [pl.BlockSpec(memory_space=pl.ANY)] * (2 * n)
        + [WHOLE] * (0 if first else 1),
        out_specs=WHOLE,
        scratch_shapes=scratch,
        compiler_params=pltpu.CompilerParams(vmem_limit_bytes=44 << 20),
        cost_estimate=pl.CostEstimate(
            flops=2 * rows * depth * columns * n,
            bytes_accessed=2 * n * depth * (rows + columns),
            transcendentals=0,
        ),
    )(owners, amps, *blocks, *([] if first else [before]))


def cycle_kernel(n, at_ref, occ_ref, low_ref, left_ref, vir_ref, *refs):
    parts, out_ref, right, sems = refs[:n], refs[n], refs[n + 1], refs[n + 2]
    rows = left_ref.shape[0]
    each = right.shape[0] // RING

    def copy(i):
        owner = (at_ref[0] + OFFSETS[i]) & (RING - 1)
        size = parts[i].shape[0]
        start = owner * each + (each // 2 if i == n - 1 else 0)
        return pltpu.make_async_copy(
            parts[i], right.at[pl.ds(pl.multiple_of(start, each // 2), size)], sems.at[i]
        )

    for i in range(n):
        copy(i).start()
    row = lax.broadcasted_iota(jnp.int32, (rows, 128), 0)
    row_label = jnp.zeros((rows, 128), jnp.int32)
    for i in range(rows // CW):
        label = occ_ref[at_ref[0] * (rows // CW) + i]
        for e in range(CW):
            row_label = jnp.where(row == i * CW + e, label ^ low_ref[e], row_label)
    count = out_ref.shape[1] // NV
    labels = [vir_ref[...] ^ occ_ref[at_ref[1] * count + j] for j in range(count)]
    col_label = jnp.concatenate(labels, axis=1)
    allowed = ((row_label[:, :1] ^ col_label) & 7) == 0
    for i in range(n):
        copy(i).wait()
    total = jnp.dot(left_ref[...], right[...], preferred_element_type=jnp.float32)
    out_ref[...] = jnp.where(allowed, total, 0.0).astype(out_ref.dtype)


def cycle_part(at, occ, vir, left, parts):
    rows, columns, depth = left.shape[0], parts[0].shape[1], left.shape[1]
    scalars = pl.BlockSpec(memory_space=pltpu.SMEM)
    return pl.pallas_call(
        functools.partial(cycle_kernel, len(parts)),
        out_shape=jax.ShapeDtypeStruct((rows, columns), jnp.bfloat16),
        in_specs=[scalars] * 3
        + [WHOLE] * 2
        + [pl.BlockSpec(memory_space=pl.ANY)] * len(parts),
        out_specs=WHOLE,
        scratch_shapes=[
            pltpu.VMEM((depth, columns), jnp.bfloat16),
            pltpu.SemaphoreType.DMA((len(parts),)),
        ],
        compiler_params=pltpu.CompilerParams(vmem_limit_bytes=16 << 20),
        cost_estimate=pl.CostEstimate(
            flops=2 * rows * depth * columns,
            bytes_accessed=2 * columns * (depth + rows),
            transcendentals=0,
        ),
    )(at, occ, vir[:CW], left, vir.reshape(1, -1), *parts)


def shards(amplitudes, integrals, cycle_integrals, occ_irrep, vir_irrep):
    rows_here, local_cols = amplitudes.shape
    occ_block = rows_here // NO
    z = lax.axis_index("row")
    p = lax.axis_index(("col", "depth"))

    padded = jnp.pad(amplitudes, ((0, 0), (0, LANES - local_cols)))
    gathered = lax.all_gather(padded, ("col", "depth"), axis=0, tiled=True)
    gathered = gathered.reshape(RING * QUARTERS, rows_here, LANES)

    half = NV // 2
    top = integrals[:half].reshape(2, half // 2, -1)
    bot = integrals[half:].reshape(2, half // 2, -1)

    tops, bots, regrouped = {0: top}, {0: bot}, {}
    for s in range(1, 5):
        tops[-s], bots[s] = shift(tops[1 - s], 1), shift(bots[s - 1], -1)
        if s < 4:
            bots[-s], tops[s] = shift(bots[1 - s], 1), shift(tops[s - 1], -1)
    tops[4] = tops.pop(-4)

    window = amplitudes.reshape(occ_block, NO, local_cols)[:, :JW, :]
    window = tie(window, [tops[-1], bots[1]])
    spread = lax.all_to_all(window, ("col", "depth"), split_axis=1, concat_axis=2, tiled=True)
    occ_here = spread.shape[1]
    columns = occ_here * NV
    ordered = (
        spread.reshape(occ_block, occ_here, CW, NV)
        .transpose(0, 2, 1, 3)
        .reshape(occ_block * CW, columns)
    )
    width = ordered.shape[0] // 2
    regrouped[0] = ordered
    regrouped[-1], regrouped[1] = shift(ordered, 1), shift(ordered, -1)
    regrouped[-1], regrouped[1] = (tie(regrouped[d], [bots[-2], tops[2]]) for d in (-1, 1))
    regrouped[-2], regrouped[2] = shift(regrouped[-1], 1), shift(regrouped[1], -1)
    regrouped[-2], regrouped[2] = (tie(regrouped[d], [tops[-3], bots[3]]) for d in (-2, 2))
    regrouped[-3], regrouped[3] = shift(regrouped[-2], 1), shift(regrouped[2], -1)
    def blocks(offsets):
        return [b for d in offsets for b in (tops[d], bots[d])]

    def owners(offsets):
        return (z + jnp.array(offsets, jnp.int32)) & (RING - 1)

    near, middle, late = [0, -1, 1, -2, 2], [-3, 3], [4]
    total = ladder_part(owners(near), gathered, blocks(near), None, False)
    regrouped[-3], regrouped[3] = (
        tie(regrouped[d], [total[:8, :128].astype(jnp.bfloat16)]) for d in (-3, 3)
    )
    regrouped[4] = [shift(regrouped[-3][:width], 1), shift(regrouped[3][width:], -1)]
    total = ladder_part(owners(middle), gathered, blocks(middle), total, False)
    ladder = ladder_part(owners(late), gathered, blocks(late), total, True)

    parts = [regrouped[d] for d in OFFSETS[:7]] + regrouped[4]
    here = jnp.stack([z, p]).astype(jnp.int32)
    cycle = cycle_part(here, occ_irrep, vir_irrep, cycle_integrals, parts)
    return ladder, cycle


def solution(mesh):
    in_specs = (P("row", ("col", "depth")), P("row", ("col", "depth")), P("row", None), P(), P())
    out_specs = (P("row", ("col", "depth")), P("row", ("col", "depth")))
    return jax.shard_map(shards, mesh=mesh, in_specs=in_specs, out_specs=out_specs, check_vma=False)
```

```python
import functools

import jax
import jax.numpy as jnp
from jax import lax
from jax.experimental import pallas as pl
from jax.experimental.pallas import tpu as pltpu
from jax.sharding import PartitionSpec as P

NO = 100
NV = 900
JW = 64
CW = 8
RING = 8
QUARTERS = 4
LANES = 256
VLIM = 16 << 20
OFFSETS = (0, -1, 1, -2, 2, -3, 3, 4, 4)
UP = [(i, (i + 1) % RING) for i in range(RING)]
DOWN = [(i, (i - 1) % RING) for i in range(RING)]
WHOLE = pl.BlockSpec(memory_space=pltpu.VMEM)


def shift(value, step):
    return lax.ppermute(value, "row", UP if step > 0 else DOWN)


def tie(value, done):
    at = (0,) * value.ndim
    size = (1,) * (value.ndim - 2) + (8, 128)
    corner = lax.slice(value, at, size)
    for other in done:
        first = lax.slice(other, (0,) * other.ndim, (1,) * (other.ndim - 2) + (8, 128))
        corner = corner + first.reshape(size) * jnp.zeros((), value.dtype)
    return lax.dynamic_update_slice(value, corner, at)


def ladder_kernel(n, first, last, owner_ref, amps_ref, *refs):
    blocks, refs = refs[: 2 * n], refs[2 * n :]
    before_ref = None
    if not first:
        before_ref, refs = refs[0], refs[1:]
    out_ref, held, halves, right, sems = refs[:5]
    total = refs[5] if last and n > 1 else out_ref

    def fetch(k):
        start = pl.multiple_of(owner_ref[k] * QUARTERS, QUARTERS)
        copies = [
            pltpu.make_async_copy(
                amps_ref.at[start + q],
                held.at[k % 2, :, pl.ds(LANES * q, LANES)],
                sems.at[k % 2, q],
            )
            for q in range(QUARTERS)
        ]
        copies += [
            pltpu.make_async_copy(blocks[2 * k + h], halves.at[k % 2, h], sems.at[k % 2, QUARTERS + h])
            for h in range(2)
        ]
        return copies

    for c in fetch(0):
        c.start()
    for k in range(n):
        if k + 1 < n:
            for c in fetch(k + 1):
                c.start()
        for c in fetch(k):
            c.wait()
        for q in range(QUARTERS):
            block = halves[k % 2, q // 2, q % 2]
            rest = jnp.zeros((LANES - block.shape[0], block.shape[1]), block.dtype)
            right[LANES * q : LANES * (q + 1), :] = jnp.concatenate([block, rest], axis=0)
        value = jnp.dot(held[k % 2], right[...], preferred_element_type=jnp.float32)
        if k > 0:
            value = value + total[...]
        elif before_ref is not None:
            value = value + before_ref[...]
        if last and k == n - 1:
            out_ref[...] = value.astype(out_ref.dtype)
        else:
            total[...] = value


def ladder_part(owners, amps, blocks, before, last):
    n = len(blocks) // 2
    rows, columns = amps.shape[1], blocks[0].shape[2]
    first = before is None
    depth = QUARTERS * LANES
    scratch = [
        pltpu.VMEM((2, rows, depth), jnp.bfloat16),
        pltpu.VMEM((2, 2) + blocks[0].shape, jnp.bfloat16),
        pltpu.VMEM((depth, columns), jnp.bfloat16),
        pltpu.SemaphoreType.DMA((2, QUARTERS + 2)),
    ]
    if last and n > 1:
        scratch.append(pltpu.VMEM((rows, columns), jnp.float32))
    return pl.pallas_call(
        functools.partial(ladder_kernel, n, first, last),
        out_shape=jax.ShapeDtypeStruct((rows, columns), jnp.bfloat16 if last else jnp.float32),
        in_specs=[pl.BlockSpec(memory_space=pltpu.SMEM), pl.BlockSpec(memory_space=pl.ANY)]
        + [pl.BlockSpec(memory_space=pl.ANY)] * (2 * n)
        + [WHOLE] * (0 if first else 1),
        out_specs=WHOLE,
        scratch_shapes=scratch,
        compiler_params=pltpu.CompilerParams(vmem_limit_bytes=44 << 20),
        cost_estimate=pl.CostEstimate(
            flops=2 * rows * depth * columns * n,
            bytes_accessed=2 * n * depth * (rows + columns),
            transcendentals=0,
        ),
    )(owners, amps, *blocks, *([] if first else [before]))


def cycle_kernel(n, at_ref, occ_ref, low_ref, left_ref, vir_ref, *refs):
    parts, out_ref, right = refs[:n], refs[n], refs[n + 1]
    rows = left_ref.shape[0]
    each = right.shape[0] // RING

    for i in range(n):
        size = parts[i].shape[0]
        owner = (at_ref[0] + OFFSETS[i]) & (RING - 1)
        start = owner * each + (each // 2 if i == n - 1 else 0)
        right[pl.ds(pl.multiple_of(start, each // 2), size), :] = parts[i][...]
    row = lax.broadcasted_iota(jnp.int32, (rows, 128), 0)
    row_label = jnp.zeros((rows, 128), jnp.int32)
    for i in range(rows // CW):
        label = occ_ref[at_ref[0] * (rows // CW) + i]
        for e in range(CW):
            row_label = jnp.where(row == i * CW + e, label ^ low_ref[e], row_label)
    count = out_ref.shape[1] // NV
    labels = [vir_ref[...] ^ occ_ref[at_ref[1] * count + j] for j in range(count)]
    col_label = jnp.concatenate(labels, axis=1)
    allowed = ((row_label[:, :1] ^ col_label) & 7) == 0
    total = jnp.dot(left_ref[...], right[...], preferred_element_type=jnp.float32)
    out_ref[...] = jnp.where(allowed, total, 0.0).astype(out_ref.dtype)


def cycle_part(at, occ, vir, left, parts):
    rows, columns, depth = left.shape[0], parts[0].shape[1], left.shape[1]
    scalars = pl.BlockSpec(memory_space=pltpu.SMEM)
    return pl.pallas_call(
        functools.partial(cycle_kernel, len(parts)),
        out_shape=jax.ShapeDtypeStruct((rows, columns), jnp.bfloat16),
        in_specs=[scalars] * 3
        + [WHOLE] * (2 + len(parts)),
        out_specs=WHOLE,
        scratch_shapes=[pltpu.VMEM((depth, columns), jnp.bfloat16)],
        compiler_params=pltpu.CompilerParams(vmem_limit_bytes=16 << 20),
        cost_estimate=pl.CostEstimate(
            flops=2 * rows * depth * columns,
            bytes_accessed=2 * columns * (depth + rows),
            transcendentals=0,
        ),
    )(at, occ, vir[:CW], left, vir.reshape(1, -1), *parts)


def shards(amplitudes, integrals, cycle_integrals, occ_irrep, vir_irrep):
    rows_here, local_cols = amplitudes.shape
    occ_block = rows_here // NO
    z = lax.axis_index("row")
    p = lax.axis_index(("col", "depth"))

    padded = jnp.pad(amplitudes, ((0, 0), (0, LANES - local_cols)))
    gathered = lax.all_gather(padded, ("col", "depth"), axis=0, tiled=True)
    gathered = gathered.reshape(RING * QUARTERS, rows_here, LANES)

    half = NV // 2
    top = integrals[:half].reshape(2, half // 2, -1)
    bot = integrals[half:].reshape(2, half // 2, -1)

    tops, bots, regrouped = {0: top}, {0: bot}, {}
    for s in range(1, 5):
        tops[-s], bots[s] = shift(tops[1 - s], 1), shift(bots[s - 1], -1)
        if s < 4:
            bots[-s], tops[s] = shift(bots[1 - s], 1), shift(tops[s - 1], -1)
    tops[4] = tops.pop(-4)

    window = amplitudes.reshape(occ_block, NO, local_cols)[:, :JW, :]
    window = tie(window, [tops[-1], bots[1]])
    spread = lax.all_to_all(window, ("col", "depth"), split_axis=1, concat_axis=2, tiled=True)
    occ_here = spread.shape[1]
    columns = occ_here * NV
    ordered = (
        spread.reshape(occ_block, occ_here, CW, NV)
        .transpose(0, 2, 1, 3)
        .reshape(occ_block * CW, columns)
    )
    width = ordered.shape[0] // 2
    regrouped[0] = ordered
    regrouped[-1], regrouped[1] = shift(ordered, 1), shift(ordered, -1)
    regrouped[-1], regrouped[1] = (tie(regrouped[d], [bots[-2], tops[2]]) for d in (-1, 1))
    regrouped[-2], regrouped[2] = shift(regrouped[-1], 1), shift(regrouped[1], -1)
    regrouped[-2], regrouped[2] = (tie(regrouped[d], [tops[-3], bots[3]]) for d in (-2, 2))
    regrouped[-3], regrouped[3] = shift(regrouped[-2], 1), shift(regrouped[2], -1)
    def blocks(offsets):
        return [b for d in offsets for b in (tops[d], bots[d])]

    def owners(offsets):
        return (z + jnp.array(offsets, jnp.int32)) & (RING - 1)

    near, middle, late = [0, -1, 1], [-2, 2, -3, 3], [4]
    total = ladder_part(owners(near), gathered, blocks(near), None, False)
    regrouped[-3], regrouped[3] = (
        tie(regrouped[d], [total[:8, :128].astype(jnp.bfloat16)]) for d in (-3, 3)
    )
    regrouped[4] = [shift(regrouped[-3][:width], 1), shift(regrouped[3][width:], -1)]
    total = ladder_part(owners(middle), gathered, blocks(middle), total, False)
    ladder = ladder_part(owners(late), gathered, blocks(late), total, True)

    parts = [regrouped[d] for d in OFFSETS[:7]] + regrouped[4]
    here = jnp.stack([z, p]).astype(jnp.int32)
    cycle = cycle_part(here, occ_irrep, vir_irrep, cycle_integrals, parts)
    return ladder, cycle


def solution(mesh):
    in_specs = (P("row", ("col", "depth")), P("row", ("col", "depth")), P("row", None), P(), P())
    out_specs = (P("row", ("col", "depth")), P("row", ("col", "depth")))
    return jax.shard_map(shards, mesh=mesh, in_specs=in_specs, out_specs=out_specs, check_vma=False)
```

```python
import functools

import jax
import jax.numpy as jnp
from jax import lax
from jax.experimental import pallas as pl
from jax.experimental.pallas import tpu as pltpu
from jax.sharding import PartitionSpec as P

NO = 100
NV = 900
JW = 64
CW = 8
RING = 8
QUARTERS = 4
LANES = 256
VLIM = 16 << 20
OFFSETS = (0, -1, 1, -2, 2, -3, 3, 4, 4)
UP = [(i, (i + 1) % RING) for i in range(RING)]
DOWN = [(i, (i - 1) % RING) for i in range(RING)]
WHOLE = pl.BlockSpec(memory_space=pltpu.VMEM)


def shift(value, step):
    return lax.ppermute(value, "row", UP if step > 0 else DOWN)


def tie(value, done):
    at = (0,) * value.ndim
    size = (1,) * (value.ndim - 2) + (8, 128)
    corner = lax.slice(value, at, size)
    for other in done:
        first = lax.slice(other, (0,) * other.ndim, (1,) * (other.ndim - 2) + (8, 128))
        corner = corner + first.reshape(size) * jnp.zeros((), value.dtype)
    return lax.dynamic_update_slice(value, corner, at)


def ladder_kernel(n, first, last, owner_ref, amps_ref, *refs):
    blocks, refs = refs[: 2 * n], refs[2 * n :]
    before_ref = None
    if not first:
        before_ref, refs = refs[0], refs[1:]
    out_ref, held, halves, right, sems = refs[:5]
    total = refs[5] if last and n > 1 else out_ref

    def fetch(k):
        start = pl.multiple_of(owner_ref[k] * QUARTERS, QUARTERS)
        copies = [
            pltpu.make_async_copy(
                amps_ref.at[start + q],
                held.at[k % 2, :, pl.ds(LANES * q, LANES)],
                sems.at[k % 2, q],
            )
            for q in range(QUARTERS)
        ]
        copies += [
            pltpu.make_async_copy(blocks[2 * k + h], halves.at[k % 2, h], sems.at[k % 2, QUARTERS + h])
            for h in range(2)
        ]
        return copies

    for c in fetch(0):
        c.start()
    for k in range(n):
        if k + 1 < n:
            for c in fetch(k + 1):
                c.start()
        for c in fetch(k):
            c.wait()
        for q in range(QUARTERS):
            block = halves[k % 2, q // 2, q % 2]
            rest = jnp.zeros((LANES - block.shape[0], block.shape[1]), block.dtype)
            right[LANES * q : LANES * (q + 1), :] = jnp.concatenate([block, rest], axis=0)
        value = jnp.dot(held[k % 2], right[...], preferred_element_type=jnp.float32)
        if k > 0:
            value = value + total[...]
        elif before_ref is not None:
            value = value + before_ref[...]
        if last and k == n - 1:
            out_ref[...] = value.astype(out_ref.dtype)
        else:
            total[...] = value


def ladder_part(owners, amps, blocks, before, last):
    n = len(blocks) // 2
    rows, columns = amps.shape[1], blocks[0].shape[2]
    first = before is None
    depth = QUARTERS * LANES
    scratch = [
        pltpu.VMEM((2, rows, depth), jnp.bfloat16),
        pltpu.VMEM((2, 2) + blocks[0].shape, jnp.bfloat16),
        pltpu.VMEM((depth, columns), jnp.bfloat16),
        pltpu.SemaphoreType.DMA((2, QUARTERS + 2)),
    ]
    if last and n > 1:
        scratch.append(pltpu.VMEM((rows, columns), jnp.float32))
    return pl.pallas_call(
        functools.partial(ladder_kernel, n, first, last),
        out_shape=jax.ShapeDtypeStruct((rows, columns), jnp.bfloat16 if last else jnp.float32),
        in_specs=[pl.BlockSpec(memory_space=pltpu.SMEM), pl.BlockSpec(memory_space=pl.ANY)]
        + [pl.BlockSpec(memory_space=pl.ANY)] * (2 * n)
        + [WHOLE] * (0 if first else 1),
        out_specs=WHOLE,
        scratch_shapes=scratch,
        compiler_params=pltpu.CompilerParams(vmem_limit_bytes=44 << 20),
        cost_estimate=pl.CostEstimate(
            flops=2 * rows * depth * columns * n,
            bytes_accessed=2 * n * depth * (rows + columns),
            transcendentals=0,
        ),
    )(owners, amps, *blocks, *([] if first else [before]))


def cycle_kernel(n, at_ref, occ_ref, low_ref, left_ref, vir_ref, *refs):
    parts, out_ref, right = refs[:n], refs[n], refs[n + 1]
    rows = left_ref.shape[0]
    each = right.shape[0] // RING

    for i in range(n):
        size = parts[i].shape[0]
        owner = (at_ref[0] + OFFSETS[i]) & (RING - 1)
        start = owner * each + (each // 2 if i == n - 1 else 0)
        right[pl.ds(pl.multiple_of(start, each // 2), size), :] = parts[i][...]
    row = lax.broadcasted_iota(jnp.int32, (rows, 128), 0)
    row_label = jnp.zeros((rows, 128), jnp.int32)
    for i in range(rows // CW):
        label = occ_ref[at_ref[0] * (rows // CW) + i]
        for e in range(CW):
            row_label = jnp.where(row == i * CW + e, label ^ low_ref[e], row_label)
    count = out_ref.shape[1] // NV
    labels = [vir_ref[...] ^ occ_ref[at_ref[1] * count + j] for j in range(count)]
    col_label = jnp.concatenate(labels, axis=1)
    allowed = ((row_label[:, :1] ^ col_label) & 7) == 0
    total = jnp.dot(left_ref[...], right[...], preferred_element_type=jnp.float32)
    out_ref[...] = jnp.where(allowed, total, 0.0).astype(out_ref.dtype)


def cycle_part(at, occ, vir, left, parts):
    rows, columns, depth = left.shape[0], parts[0].shape[1], left.shape[1]
    scalars = pl.BlockSpec(memory_space=pltpu.SMEM)
    return pl.pallas_call(
        functools.partial(cycle_kernel, len(parts)),
        out_shape=jax.ShapeDtypeStruct((rows, columns), jnp.bfloat16),
        in_specs=[scalars] * 3
        + [WHOLE] * (2 + len(parts)),
        out_specs=WHOLE,
        scratch_shapes=[pltpu.VMEM((depth, columns), jnp.bfloat16)],
        compiler_params=pltpu.CompilerParams(vmem_limit_bytes=16 << 20),
        cost_estimate=pl.CostEstimate(
            flops=2 * rows * depth * columns,
            bytes_accessed=2 * columns * (depth + rows),
            transcendentals=0,
        ),
    )(at, occ, vir[:CW], left, vir.reshape(1, -1), *parts)


def shards(amplitudes, integrals, cycle_integrals, occ_irrep, vir_irrep):
    rows_here, local_cols = amplitudes.shape
    occ_block = rows_here // NO
    z = lax.axis_index("row")
    p = lax.axis_index(("col", "depth"))

    padded = jnp.pad(amplitudes, ((0, 0), (0, LANES - local_cols)))
    gathered = lax.all_gather(padded, ("col", "depth"), axis=0, tiled=True)
    gathered = gathered.reshape(RING * QUARTERS, rows_here, LANES)

    half = NV // 2
    top = integrals[:half].reshape(2, half // 2, -1)
    bot = integrals[half:].reshape(2, half // 2, -1)

    tops, bots, regrouped = {0: top}, {0: bot}, {}
    for s in range(1, 5):
        tops[-s], bots[s] = shift(tops[1 - s], 1), shift(bots[s - 1], -1)
        if s < 4:
            bots[-s], tops[s] = shift(bots[1 - s], 1), shift(tops[s - 1], -1)
    tops[4] = tops.pop(-4)

    window = amplitudes.reshape(occ_block, NO, local_cols)[:, :JW, :]
    window = tie(window, [tops[-1], bots[1]])
    spread = lax.all_to_all(window, ("col", "depth"), split_axis=1, concat_axis=2, tiled=True)
    occ_here = spread.shape[1]
    columns = occ_here * NV
    ordered = (
        spread.reshape(occ_block, occ_here, CW, NV)
        .transpose(0, 2, 1, 3)
        .reshape(occ_block * CW, columns)
    )
    width = ordered.shape[0] // 2
    regrouped[0] = ordered
    regrouped[-1], regrouped[1] = shift(ordered, 1), shift(ordered, -1)
    regrouped[-1], regrouped[1] = (tie(regrouped[d], [bots[-2], tops[2]]) for d in (-1, 1))
    regrouped[-2], regrouped[2] = shift(regrouped[-1], 1), shift(regrouped[1], -1)
    regrouped[-2], regrouped[2] = (tie(regrouped[d], [tops[-3], bots[3]]) for d in (-2, 2))
    regrouped[-3], regrouped[3] = shift(regrouped[-2], 1), shift(regrouped[2], -1)
    def blocks(offsets):
        return [b for d in offsets for b in (tops[d], bots[d])]

    def owners(offsets):
        return (z + jnp.array(offsets, jnp.int32)) & (RING - 1)

    near, middle, late = [0, -1], [1, -2, 2, -3, 3], [4]
    total = ladder_part(owners(near), gathered, blocks(near), None, False)
    regrouped[-3], regrouped[3] = (
        tie(regrouped[d], [total[:8, :128].astype(jnp.bfloat16)]) for d in (-3, 3)
    )
    regrouped[4] = [shift(regrouped[-3][:width], 1), shift(regrouped[3][width:], -1)]
    total = ladder_part(owners(middle), gathered, blocks(middle), total, False)
    ladder = ladder_part(owners(late), gathered, blocks(late), total, True)

    parts = [regrouped[d] for d in OFFSETS[:7]] + regrouped[4]
    here = jnp.stack([z, p]).astype(jnp.int32)
    cycle = cycle_part(here, occ_irrep, vir_irrep, cycle_integrals, parts)
    return ladder, cycle


def solution(mesh):
    in_specs = (P("row", ("col", "depth")), P("row", ("col", "depth")), P("row", None), P(), P())
    out_specs = (P("row", ("col", "depth")), P("row", ("col", "depth")))
    return jax.shard_map(shards, mesh=mesh, in_specs=in_specs, out_specs=out_specs, check_vma=False)
```
